32 devices in a mesh: rep: 2 (over core), fsdp: 16 (over z, y, x).
Axes of the slice: x: 2, y: 2, z: 4, core: 2. Of those that a mesh axis runs over, the one named last changes fastest.
Arguments:
- attn_out: bfloat16 [49152, 512], P(('rep', 'fsdp')), may hold values from -6 to 6
- cotangent: bfloat16 [49152, 1024], P(('rep', 'fsdp')), may hold values from -6 to 6
- numer: float32 [2, 1024, 512], P('rep', 'fsdp'), may hold values from -6 to 6
- push_weight: float32 [2], P('rep'), may hold values from 0.5 to 2
- moment1: float32 [2, 1024, 512], P('rep', 'fsdp'), may hold values from -0.06 to 0.06
- moment2: float32 [2, 1024, 512], P('rep', 'fsdp'), may hold values from 1e-05 to 0.001
- step_index: int32 [1], replicated, may hold values from 0 to 7
- token_count: int32 [2], P('rep'), may hold values from 12288 to 24576
Outputs:
- mixed_numer: float32 [2, 1024, 512], P('rep', 'fsdp')
- mixed_weight: float32 [2], P('rep')
- new_moment1: float32 [2, 1024, 512], P('rep', 'fsdp')
- new_moment2: float32 [2, 1024, 512], P('rep', 'fsdp')
The draws below stay inside these ranges and needn't reach their ends.
All inputs are finite; a program needn't handle non-finite values.
Results may differ from the reference program's by a relative error of at most 0.0003.
Values sent between devices are 32-bit elements; how exact they have to be, the bound alone decides.
No kernel may reach another device: no remote copies, remote signals or barrier semaphores. Data moves between devices by JAX's collectives and lax.ppermute only.
A program may use at most 64 MiB of HBM per device.

```python
import math
import jax
import jax.numpy as jnp

SLAB_OUT = 1024
TOK_DEV = 1536
SLAB_IN = 512
REP_TOKENS = 24576
TOKENS = 49152
N_REP = 2
N_FSDP = 16


def strengthened(entries, key, source, target, blocks, factor):
    owner, partner = [(jnp.arange(entries.shape[dim]) // (entries.shape[dim] // blocks)).reshape([-1 if axis == dim else 1 for axis in range(entries.ndim)]) for dim in (source, target)]
    chosen = jax.random.permutation(key, blocks)[partner]
    strong = (owner == chosen) | (owner == (partner + blocks // 2) % blocks)
    return jnp.where(strong, factor * entries, entries)


def steps_of(stream_key, dims, pieces, least, high):
    def one(dim, parts):
        heights = jax.random.uniform(jax.random.fold_in(jax.random.fold_in(stream_key, 6), dim), (parts,), jnp.float32, least / len(pieces), high / len(pieces))
        return jnp.repeat(jnp.exp(heights), dims[dim] // parts).reshape((-1,) + (1,) * (len(dims) - dim - 1))

    loudness = one(*pieces[0])
    for cut in pieces[1:]:
        loudness = loudness * one(*cut)
    return loudness


def noise(stream_key, extent, width, reach, pieces=(), kind=jnp.bfloat16):
    level = steps_of(stream_key, extent, pieces, -0.22, 0.18) if pieces else 1.0
    entries = jax.random.normal(stream_key, extent, jnp.float32) * width * level
    return jnp.minimum(jnp.maximum(entries, -reach), reach).astype(kind)


def gaussian_with(key, dims, width, most, shards, heavy, kind=jnp.bfloat16):
    values = width * jax.random.normal(key, dims, jnp.float32)
    if shards:
        values = values * steps_of(key, dims, shards, -0.22, 0.18)
    return jnp.clip(strengthened(values, jax.random.fold_in(key, 3), *heavy), -most, most).astype(kind)


def setup_inputs(seed: int = 0) -> dict:
    streams_of = jax.random.split(jax.random.key(seed), 9)
    return {
        "attn_out": noise(streams_of[0], (TOKENS, SLAB_IN), 1.0, 6.0, ((0, 32),)),
        "cotangent": gaussian_with(streams_of[1], (TOKENS, SLAB_OUT), 1.0, 6.0, ((0, 32),), (0, 1, 32, 2.75)),
        "numer": noise(streams_of[2], (N_REP, SLAB_OUT, SLAB_IN), 1.0, 6.0, ((0, 2), (1, 16)), jnp.float32),
        "push_weight": jnp.clip(jnp.exp(math.log(2.0) - 1.3862944 * jax.random.uniform(streams_of[3], (N_REP,), jnp.float32) ** steps_of(streams_of[3], (N_REP,), ((0, 2),), -0.2, 0.2)), 0.5, 2.0),
        "moment1": noise(streams_of[4], (N_REP, SLAB_OUT, SLAB_IN), 0.01, 0.06, ((0, 2), (1, 16)), jnp.float32),
        "moment2": jnp.clip(jnp.exp(math.log(0.001) - 4.6051703 * jax.random.uniform(streams_of[5], (N_REP, SLAB_OUT, SLAB_IN), jnp.float32) ** steps_of(streams_of[5], (N_REP, SLAB_OUT, SLAB_IN), ((0, 2), (1, 16)), -0.2, 0.2)), 9.999999747378752e-06, 0.001),
        "step_index": jax.random.randint(streams_of[6], (1,), 0, 8).astype(jnp.int32),
        "token_count": jax.random.randint(streams_of[7], (N_REP,), REP_TOKENS // 2, REP_TOKENS + 1).astype(jnp.int32),
    }


def reference(attn_out, cotangent, numer, push_weight, moment1, moment2, step_index, token_count):
    group_rows = TOK_DEV * N_FSDP
    bit_count = int(N_REP).bit_length() - 1
    step = step_index[0]
    bit = step % bit_count
    t_value = (step + 1).astype(jnp.float32)
    grads = []
    for group in range(N_REP):
        inputs = attn_out[group * group_rows:(group + 1) * group_rows]
        outgrad = cotangent[group * group_rows:(group + 1) * group_rows]
        position = jnp.arange(group_rows, dtype=jnp.int32)
        masked = jnp.where((position < token_count[group])[:, None], inputs, jnp.zeros_like(inputs))
        total = jnp.dot(outgrad.T, masked, preferred_element_type=jnp.float32)
        grads.append(total / token_count[group].astype(jnp.float32))
    grad = jnp.stack(grads, axis=0)
    beta_one = jnp.float32(0.9)
    beta_two = jnp.float32(0.95)
    new_moment1 = beta_one * moment1 + (1.0 - beta_one) * grad
    new_moment2 = beta_two * moment2 + (1.0 - beta_two) * grad * grad
    weight_col = push_weight[:, None, None]
    debiased = numer / weight_col
    first_hat = new_moment1 / (1.0 - jnp.power(beta_one, t_value))
    second_hat = new_moment2 / (1.0 - jnp.power(beta_two, t_value))
    update = first_hat / (jnp.sqrt(second_hat) + 1e-08) + 0.1 * debiased
    stepped = numer - 0.02 * weight_col * update
    partner = jnp.bitwise_xor(jnp.arange(N_REP, dtype=jnp.int32), jnp.left_shift(jnp.int32(1), bit))
    mixed_numer = 0.75 * stepped + 0.25 * stepped[partner]
    mixed_weight = 0.75 * push_weight + 0.25 * push_weight[partner]
    return (mixed_numer, mixed_weight, new_moment1, new_moment2)
```

```python
import functools
import jax
import jax.numpy as jnp
from jax import lax
from jax.experimental import pallas as pl
from jax.experimental.pallas import tpu as pltpu
from jax.sharding import PartitionSpec as P

ORDERS = (
    ((4, 2, 1, 8), (2, 1, 8, 4)),
    ((1, 8, 4, 2), (1, 4, 2, 8)),
)
SHARE = 0.625


def orders_of(size):
    if size == 16:
        return ORDERS
    bits = tuple(1 << k for k in range(size.bit_length() - 1))
    turned = bits[1:] + bits[:1]
    return ((bits, turned), (bits[::-1], turned[::-1]))


def rows_of(owned):
    first = min(max(8, 8 * round(SHARE * owned / 8)), owned - 8)
    return (first, owned - first)


def place(relative, order):
    top = len(order) - 1
    spot = 0
    for k, bit in enumerate(order):
        low = bit.bit_length() - 1
        spot = spot | (((relative >> low) & 1) << (top - k))
    return spot


def product_kernel(orders, rows, owned, tok_rows, group, info, attn, cot, *rest):
    outs, masked = rest[:4], rest[4]
    me, core, count = info[0], info[1], info[2]
    step = pl.program_id(0)

    @pl.when(step == 0)
    def _():
        position = me * tok_rows + lax.broadcasted_iota(jnp.int32, attn.shape, 0)
        live = position < count
        masked[...] = jnp.where(live, attn[...].astype(jnp.float32), 0.0).astype(masked.dtype)

    result = lax.dot_general(
        cot[...], masked[...], (((0,), (0,)), ((), ())), preferred_element_type=jnp.float32
    )
    half = 1 << (len(orders[0][0]) - 1)
    for s in range(group):
        relative = me ^ (step * group + s)
        base = s * owned
        for c, (even, odd) in enumerate(orders):
            spot = jnp.where(core == 0, place(relative, even), place(relative, odd))
            piece = result[base:base + rows[c]]
            base += rows[c]

            @pl.when(spot >= half)
            def _():
                outs[2 * c][spot - half] = piece

            @pl.when(spot < half)
            def _():
                outs[2 * c + 1][spot] = piece


def product(attn_out, cotangent, me, core, count, orders, rows):
    tok_rows, width = attn_out.shape
    owned = sum(rows)
    devices = cotangent.shape[1] // owned
    group = max(1, 256 // owned)
    info = jnp.stack([me, core, count])
    half = devices // 2
    return pl.pallas_call(
        functools.partial(product_kernel, orders, rows, owned, tok_rows, group),
        out_shape=[
            jax.ShapeDtypeStruct((half, r, width), jnp.float32) for r in rows for _ in range(2)
        ],
        grid_spec=pltpu.PrefetchScalarGridSpec(
            num_scalar_prefetch=1,
            grid=(devices // group,),
            in_specs=[
                pl.BlockSpec((tok_rows, width), lambda i, s: (0, 0)),
                pl.BlockSpec((tok_rows, group * owned), lambda i, s: (0, i)),
            ],
            out_specs=[
                pl.BlockSpec((half, r, width), lambda i, s: (0, 0, 0))
                for r in rows for _ in range(2)
            ],
            scratch_shapes=[pltpu.VMEM((tok_rows, width), jnp.bfloat16)],
        ),
        compiler_params=pltpu.CompilerParams(vmem_limit_bytes=40 * 1024 * 1024),
        cost_estimate=pl.CostEstimate(
            flops=2 * tok_rows * width * cotangent.shape[1],
            bytes_accessed=2 * tok_rows * (width + cotangent.shape[1]) + 4 * width * cotangent.shape[1],
            transcendentals=0,
        ),
    )(info, attn_out, cotangent)


def swap(value, pair, reps, devices):
    pairs = [
        (r * devices + f, r * devices + (f ^ pair[r % 2]))
        for r in range(reps) for f in range(devices)
    ]
    return lax.ppermute(value, ("rep", "fsdp"), pairs)


def local(attn_out, cotangent, numer, push_weight, moment1, moment2, step_index, token_count):
    owned = numer.shape[1]
    reps, devices = lax.axis_size("rep"), lax.axis_size("fsdp")
    count = token_count[0]
    me, core = lax.axis_index("fsdp"), lax.axis_index("rep") % 2
    orders, rows = orders_of(devices), rows_of(owned)
    blocks = product(attn_out, cotangent, me, core, count, orders, rows)

    send, keep = list(blocks[0::2]), list(blocks[1::2])
    stages = devices.bit_length() - 1
    for k in range(stages):
        got = [swap(send[c], (orders[c][0][k], orders[c][1][k]), reps, devices) for c in range(2)]
        for c in range(2):
            if k < stages - 1:
                half = keep[c].shape[0] // 2
                send[c] = keep[c][half:] + got[c][half:]
                keep[c] = keep[c][:half] + got[c][:half]
            else:
                keep[c] = keep[c] + got[c]
    total = jnp.concatenate([keep[0], keep[1]], axis=1)
    grad = total / count.astype(jnp.float32)
    step = step_index[0]
    t_value = (step + 1).astype(jnp.float32)
    beta_one = jnp.float32(0.9)
    beta_two = jnp.float32(0.95)
    new_moment1 = beta_one * moment1 + (1.0 - beta_one) * grad
    new_moment2 = beta_two * moment2 + (1.0 - beta_two) * grad * grad
    weight_col = push_weight[:, None, None]
    debiased = numer / weight_col
    first_hat = new_moment1 / (1.0 - jnp.power(beta_one, t_value))
    second_hat = new_moment2 / (1.0 - jnp.power(beta_two, t_value))
    update = first_hat / (jnp.sqrt(second_hat) + 1e-08) + 0.1 * debiased
    stepped = numer - 0.02 * weight_col * update

    def exchange(bit, values):
        pairs = [(r, r ^ (1 << bit)) for r in range(reps)]
        return tuple(lax.ppermute(v, "rep", pairs) for v in values)

    bit_count = reps.bit_length() - 1
    if bit_count == 1:
        (mate_weight,) = exchange(0, (push_weight,))
        (mate_numer,) = exchange(0, (stepped,))
    else:
        mate_weight, mate_numer = lax.switch(
            step % bit_count,
            [functools.partial(exchange, b) for b in range(bit_count)],
            (push_weight, stepped),
        )
    mixed_numer = 0.75 * stepped + 0.25 * mate_numer
    mixed_weight = 0.75 * push_weight + 0.25 * mate_weight
    return (mixed_numer, mixed_weight, new_moment1, new_moment2)


def solution(mesh):
    placed = (
        P(("rep", "fsdp"), None),
        P(("rep", "fsdp"), None),
        P("rep", "fsdp", None),
        P("rep"),
        P("rep", "fsdp", None),
        P("rep", "fsdp", None),
        P(),
        P("rep"),
    )
    return jax.shard_map(
        local,
        mesh=mesh,
        in_specs=placed,
        out_specs=(
            P("rep", "fsdp", None),
            P("rep"),
            P("rep", "fsdp", None),
            P("rep", "fsdp", None),
        ),
        check_vma=False,
    )
```

```python
import functools
import jax
import jax.numpy as jnp
from jax import lax
from jax.experimental import pallas as pl
from jax.experimental.pallas import tpu as pltpu
from jax.sharding import PartitionSpec as P

ORDERS = (
    ((4, 1, 8, 2), (1, 2, 8, 4)),
    ((4, 2, 1, 8), (2, 1, 4, 8)),
)
SHARE = 0.5


def orders_of(size):
    if size == 16:
        return ORDERS
    bits = tuple(1 << k for k in range(size.bit_length() - 1))
    turned = bits[1:] + bits[:1]
    return ((bits, turned), (bits[::-1], turned[::-1]))


def rows_of(owned):
    first = min(max(8, 8 * round(SHARE * owned / 8)), owned - 8)
    return (first, owned - first)


def place(relative, order):
    top = len(order) - 1
    spot = 0
    for k, bit in enumerate(order):
        low = bit.bit_length() - 1
        spot = spot | (((relative >> low) & 1) << (top - k))
    return spot


def product_kernel(orders, rows, owned, slabs, columns, count, attn, cot, *rest):
    outs = rest[:len(orders)]
    attn_v, cot_v, total, attn_sems, cot_sems = rest[len(orders):]
    tok_rows, width = attn.shape
    me, core = lax.axis_index("fsdp"), lax.axis_index("rep") % 2
    depth = tok_rows // slabs
    spans = [pl.ds(k * depth, depth) for k in range(slabs)]
    attn_in = [
        pltpu.make_async_copy(attn.at[span], attn_v.at[span], attn_sems.at[k])
        for k, span in enumerate(spans)
    ]
    cot_in = [
        pltpu.make_async_copy(cot.at[span], cot_v.at[span], cot_sems.at[k])
        for k, span in enumerate(spans)
    ]
    for k in range(slabs):
        attn_in[k].start()
        cot_in[k].start()
    live = count[0] - me * tok_rows

    def put(first, result):
        for s in range(columns // owned):
            relative = me ^ (first // owned + s)
            base = s * owned
            for c, (even, odd) in enumerate(orders):
                spot = jnp.where(core == 0, place(relative, even), place(relative, odd))
                outs[c][spot] = result[base:base + rows[c]]
                base += rows[c]

    for k, span in enumerate(spans):
        attn_in[k].wait()

        @pl.when(live < (k + 1) * depth)
        def _():
            position = k * depth + lax.broadcasted_iota(jnp.int32, (depth, width), 0)
            kept = jnp.where(position < live, attn_v[span].astype(jnp.float32), 0.0)
            attn_v[span] = kept.astype(attn_v.dtype)

        cot_in[k].wait()
        for first in range(0, cot.shape[1], columns):
            part = pl.ds(first, columns)
            term = lax.dot_general(
                cot_v[span, part], attn_v[span], (((0,), (0,)), ((), ())),
                preferred_element_type=jnp.float32,
            )
            if k > 0:
                term = total[part] + term
            if k < slabs - 1:
                total[part] = term
            else:
                put(first, term)


def product(attn_out, cotangent, token_count, orders, rows):
    tok_rows, width = attn_out.shape
    owned = sum(rows)
    features = cotangent.shape[1]
    slabs = 6 if tok_rows % 96 == 0 else 1
    far = [pltpu.with_memory_space_constraint(v, pltpu.HBM) for v in (attn_out, cotangent)]
    return pl.pallas_call(
        functools.partial(product_kernel, orders, rows, owned, slabs, max(256, owned)),
        out_shape=[
            jax.ShapeDtypeStruct((features // owned, r, width), jnp.float32) for r in rows
        ],
        in_specs=[pl.BlockSpec(memory_space=pltpu.SMEM)] + [pl.BlockSpec(memory_space=pltpu.HBM)] * 2,
        out_specs=[pl.BlockSpec(memory_space=pltpu.VMEM)] * len(rows),
        scratch_shapes=[
            pltpu.VMEM((tok_rows, width), attn_out.dtype),
            pltpu.VMEM((tok_rows, features), cotangent.dtype),
            pltpu.VMEM((features, width), jnp.float32),
            pltpu.SemaphoreType.DMA((slabs,)),
            pltpu.SemaphoreType.DMA((slabs,)),
        ],
        compiler_params=pltpu.CompilerParams(vmem_limit_bytes=32 * 1024 * 1024),
        cost_estimate=pl.CostEstimate(
            flops=2 * tok_rows * width * features,
            bytes_accessed=2 * tok_rows * (width + features) + 4 * width * features,
            transcendentals=0,
        ),
    )(token_count, *far)


def swap(value, pair, reps, devices):
    pairs = [
        (r * devices + f, r * devices + (f ^ pair[r % 2]))
        for r in range(reps) for f in range(devices)
    ]
    return lax.ppermute(value, ("rep", "fsdp"), pairs)


def local(attn_out, cotangent, numer, push_weight, moment1, moment2, step_index, token_count):
    owned = numer.shape[1]
    reps, devices = lax.axis_size("rep"), lax.axis_size("fsdp")
    count = token_count[0]
    orders, rows = orders_of(devices), rows_of(owned)
    blocks = product(attn_out, cotangent, token_count, orders, rows)

    send, keep = [b[devices // 2:] for b in blocks], [b[:devices // 2] for b in blocks]
    def mate_of(value):
        def exchange(bit, v):
            return lax.ppermute(v, "rep", [(r, r ^ (1 << bit)) for r in range(reps)])

        bit_count = reps.bit_length() - 1
        if bit_count == 1:
            return exchange(0, value)
        return lax.switch(
            step_index[0] % bit_count,
            [functools.partial(exchange, b) for b in range(bit_count)],
            value,
        )

    stages = devices.bit_length() - 1
    mixed_weight = 0.75 * push_weight + 0.25 * mate_of(push_weight)
    for k in range(stages):
        got = [swap(send[c], (orders[c][0][k], orders[c][1][k]), reps, devices) for c in range(len(orders))]
        if k == 0:
            got[0], mixed_weight = lax.optimization_barrier((got[0], mixed_weight))
        for c in range(len(orders)):
            if k < stages - 1:
                half = keep[c].shape[0] // 2
                send[c] = keep[c][half:] + got[c][half:]
                keep[c] = keep[c][:half] + got[c][:half]
            else:
                keep[c] = keep[c] + got[c]
    total = jnp.concatenate(keep, axis=1)
    grad = total / count.astype(jnp.float32)
    step = step_index[0]
    t_value = (step + 1).astype(jnp.float32)
    beta_one = jnp.float32(0.9)
    beta_two = jnp.float32(0.95)
    new_moment1 = beta_one * moment1 + (1.0 - beta_one) * grad
    new_moment2 = beta_two * moment2 + (1.0 - beta_two) * grad * grad
    weight_col = push_weight[:, None, None]
    debiased = numer / weight_col
    first_hat = new_moment1 / (1.0 - jnp.power(beta_one, t_value))
    second_hat = new_moment2 / (1.0 - jnp.power(beta_two, t_value))
    update = first_hat / (jnp.sqrt(second_hat) + 1e-08) + 0.1 * debiased
    stepped = numer - 0.02 * weight_col * update

    mate_numer = mate_of(stepped)
    mixed_numer = 0.75 * stepped + 0.25 * mate_numer
    return (mixed_numer, mixed_weight, new_moment1, new_moment2)


def solution(mesh):
    placed = (
        P(("rep", "fsdp"), None),
        P(("rep", "fsdp"), None),
        P("rep", "fsdp", None),
        P("rep"),
        P("rep", "fsdp", None),
        P("rep", "fsdp", None),
        P(),
        P("rep"),
    )
    return jax.shard_map(
        local,
        mesh=mesh,
        in_specs=placed,
        out_specs=(
            P("rep", "fsdp", None),
            P("rep"),
            P("rep", "fsdp", None),
            P("rep", "fsdp", None),
        ),
        check_vma=False,
    )
```

```python
import functools
import jax
import jax.numpy as jnp
from jax import lax
from jax.experimental import pallas as pl
from jax.experimental.pallas import tpu as pltpu
from jax.sharding import PartitionSpec as P

ORDERS = (
    ((1, 2, 4, 8), (8, 2, 1, 4)),
    ((2, 4, 8, 1), (4, 1, 2, 8)),
)
SHARE = 0.5


def orders_of(size):
    if size == 16:
        return ORDERS
    bits = tuple(1 << k for k in range(size.bit_length() - 1))
    turned = bits[1:] + bits[:1]
    return ((bits, turned), (bits[::-1], turned[::-1]))


def rows_of(owned):
    first = min(max(8, 8 * round(SHARE * owned / 8)), owned - 8)
    return (first, owned - first)


def place(relative, order):
    top = len(order) - 1
    spot = 0
    for k, bit in enumerate(order):
        low = bit.bit_length() - 1
        spot = spot | (((relative >> low) & 1) << (top - k))
    return spot


def product_kernel(orders, rows, owned, slabs, columns, count, attn, cot, *rest):
    outs = rest[:len(orders)]
    attn_v, cot_v, total, attn_sems, cot_sems = rest[len(orders):]
    tok_rows, width = attn.shape
    me, core = lax.axis_index("fsdp"), lax.axis_index("rep") % 2
    depth = tok_rows // slabs
    spans = [pl.ds(k * depth, depth) for k in range(slabs)]
    attn_in = [
        pltpu.make_async_copy(attn.at[span], attn_v.at[span], attn_sems.at[k])
        for k, span in enumerate(spans)
    ]
    cot_in = [
        pltpu.make_async_copy(cot.at[span], cot_v.at[span], cot_sems.at[k])
        for k, span in enumerate(spans)
    ]
    for k in range(slabs):
        attn_in[k].start()
        cot_in[k].start()
    live = count[0] - me * tok_rows

    def put(first, result):
        for s in range(columns // owned):
            relative = me ^ (first // owned + s)
            base = s * owned
            for c, (even, odd) in enumerate(orders):
                spot = jnp.where(core == 0, place(relative, even), place(relative, odd))
                outs[c][spot] = result[base:base + rows[c]]
                base += rows[c]

    for k, span in enumerate(spans):
        attn_in[k].wait()

        @pl.when(live < (k + 1) * depth)
        def _():
            position = k * depth + lax.broadcasted_iota(jnp.int32, (depth, width), 0)
            kept = jnp.where(position < live, attn_v[span].astype(jnp.float32), 0.0)
            attn_v[span] = kept.astype(attn_v.dtype)

        cot_in[k].wait()
        for first in range(0, cot.shape[1], columns):
            part = pl.ds(first, columns)
            term = lax.dot_general(
                cot_v[span, part], attn_v[span], (((0,), (0,)), ((), ())),
                preferred_element_type=jnp.float32,
            )
            if k > 0:
                term = total[part] + term
            if k < slabs - 1:
                total[part] = term
            else:
                put(first, term)


def product(attn_out, cotangent, token_count, orders, rows):
    tok_rows, width = attn_out.shape
    owned = sum(rows)
    features = cotangent.shape[1]
    slabs = 6 if tok_rows % 96 == 0 else 1
    far = [pltpu.with_memory_space_constraint(v, pltpu.HBM) for v in (attn_out, cotangent)]
    return pl.pallas_call(
        functools.partial(product_kernel, orders, rows, owned, slabs, max(256, owned)),
        out_shape=[
            jax.ShapeDtypeStruct((features // owned, r, width), jnp.float32) for r in rows
        ],
        in_specs=[pl.BlockSpec(memory_space=pltpu.SMEM)] + [pl.BlockSpec(memory_space=pltpu.HBM)] * 2,
        out_specs=[pl.BlockSpec(memory_space=pltpu.VMEM)] * len(rows),
        scratch_shapes=[
            pltpu.VMEM((tok_rows, width), attn_out.dtype),
            pltpu.VMEM((tok_rows, features), cotangent.dtype),
            pltpu.VMEM((features, width), jnp.float32),
            pltpu.SemaphoreType.DMA((slabs,)),
            pltpu.SemaphoreType.DMA((slabs,)),
        ],
        compiler_params=pltpu.CompilerParams(vmem_limit_bytes=32 * 1024 * 1024),
        cost_estimate=pl.CostEstimate(
            flops=2 * tok_rows * width * features,
            bytes_accessed=2 * tok_rows * (width + features) + 4 * width * features,
            transcendentals=0,
        ),
    )(token_count, *far)


def swap(value, pair, reps, devices):
    pairs = [
        (r * devices + f, r * devices + (f ^ pair[r % 2]))
        for r in range(reps) for f in range(devices)
    ]
    return lax.ppermute(value, ("rep", "fsdp"), pairs)


def local(attn_out, cotangent, numer, push_weight, moment1, moment2, step_index, token_count):
    owned = numer.shape[1]
    reps, devices = lax.axis_size("rep"), lax.axis_size("fsdp")
    count = token_count[0]
    orders, rows = orders_of(devices), rows_of(owned)
    blocks = product(attn_out, cotangent, token_count, orders, rows)

    send, keep = [b[devices // 2:] for b in blocks], [b[:devices // 2] for b in blocks]
    def mate_of(value):
        def exchange(bit, v):
            return lax.ppermute(v, "rep", [(r, r ^ (1 << bit)) for r in range(reps)])

        bit_count = reps.bit_length() - 1
        if bit_count == 1:
            return exchange(0, value)
        return lax.switch(
            step_index[0] % bit_count,
            [functools.partial(exchange, b) for b in range(bit_count)],
            value,
        )

    stages = devices.bit_length() - 1
    mixed_weight = 0.75 * push_weight + 0.25 * mate_of(push_weight)
    for k in range(stages):
        got = [swap(send[c], (orders[c][0][k], orders[c][1][k]), reps, devices) for c in range(len(orders))]
        if k == 0:
            got[0], mixed_weight = lax.optimization_barrier((got[0], mixed_weight))
        for c in range(len(orders)):
            if k < stages - 1:
                half = keep[c].shape[0] // 2
                send[c] = keep[c][half:] + got[c][half:]
                keep[c] = keep[c][:half] + got[c][:half]
            else:
                keep[c] = keep[c] + got[c]
    total = jnp.concatenate(keep, axis=1)
    grad = total / count.astype(jnp.float32)
    step = step_index[0]
    t_value = (step + 1).astype(jnp.float32)
    beta_one = jnp.float32(0.9)
    beta_two = jnp.float32(0.95)
    new_moment1 = beta_one * moment1 + (1.0 - beta_one) * grad
    new_moment2 = beta_two * moment2 + (1.0 - beta_two) * grad * grad
    weight_col = push_weight[:, None, None]
    debiased = numer / weight_col
    first_hat = new_moment1 / (1.0 - jnp.power(beta_one, t_value))
    second_hat = new_moment2 / (1.0 - jnp.power(beta_two, t_value))
    update = first_hat / (jnp.sqrt(second_hat) + 1e-08) + 0.1 * debiased
    stepped = numer - 0.02 * weight_col * update

    mate_numer = mate_of(stepped)
    mixed_numer = 0.75 * stepped + 0.25 * mate_numer
    return (mixed_numer, mixed_weight, new_moment1, new_moment2)


def solution(mesh):
    placed = (
        P(("rep", "fsdp"), None),
        P(("rep", "fsdp"), None),
        P("rep", "fsdp", None),
        P("rep"),
        P("rep", "fsdp", None),
        P("rep", "fsdp", None),
        P(),
        P("rep"),
    )
    return jax.shard_map(
        local,
        mesh=mesh,
        in_specs=placed,
        out_specs=(
            P("rep", "fsdp", None),
            P("rep"),
            P("rep", "fsdp", None),
            P("rep", "fsdp", None),
        ),
        check_vma=False,
    )
```

```python
import functools
import jax
import jax.numpy as jnp
from jax import lax
from jax.experimental import pallas as pl
from jax.experimental.pallas import tpu as pltpu
from jax.sharding import PartitionSpec as P

ORDERS = (
    ((1, 2, 4, 8), (4, 1, 2, 8)),
    ((2, 4, 1, 8), (8, 2, 1, 4)),
)
SHARE = 0.5


def orders_of(size):
    if size == 16:
        return ORDERS
    bits = tuple(1 << k for k in range(size.bit_length() - 1))
    turned = bits[1:] + bits[:1]
    return ((bits, turned), (bits[::-1], turned[::-1]))


def rows_of(owned):
    first = min(max(8, 8 * round(SHARE * owned / 8)), owned - 8)
    return (first, owned - first)


def place(relative, order):
    top = len(order) - 1
    spot = 0
    for k, bit in enumerate(order):
        low = bit.bit_length() - 1
        spot = spot | (((relative >> low) & 1) << (top - k))
    return spot


def product_kernel(orders, rows, owned, slabs, columns, count, attn, cot, *rest):
    outs = rest[:len(orders)]
    attn_v, cot_v, total, attn_sems, cot_sems = rest[len(orders):]
    tok_rows, width = attn.shape
    me, core = lax.axis_index("fsdp"), lax.axis_index("rep") % 2
    depth = tok_rows // slabs
    spans = [pl.ds(k * depth, depth) for k in range(slabs)]
    attn_in = [
        pltpu.make_async_copy(attn.at[span], attn_v.at[span], attn_sems.at[k])
        for k, span in enumerate(spans)
    ]
    cot_in = [
        pltpu.make_async_copy(cot.at[span], cot_v.at[span], cot_sems.at[k])
        for k, span in enumerate(spans)
    ]
    for k in range(slabs):
        attn_in[k].start()
        cot_in[k].start()
    live = count[0] - me * tok_rows

    def put(first, result):
        for s in range(columns // owned):
            relative = me ^ (first // owned + s)
            base = s * owned
            for c, (even, odd) in enumerate(orders):
                spot = jnp.where(core == 0, place(relative, even), place(relative, odd))
                outs[c][spot] = result[base:base + rows[c]]
                base += rows[c]

    for k, span in enumerate(spans):
        attn_in[k].wait()

        @pl.when(live <= k * depth)
        def _():
            attn_v[span] = jnp.zeros((depth, width), attn_v.dtype)

        @pl.when((live > k * depth) & (live < (k + 1) * depth))
        def _():
            position = k * depth + lax.broadcasted_iota(jnp.int32, (depth, width), 0)
            kept = jnp.where(position < live, attn_v[span].astype(jnp.float32), 0.0)
            attn_v[span] = kept.astype(attn_v.dtype)

        cot_in[k].wait()
        for first in range(0, cot.shape[1], columns):
            part = pl.ds(first, columns)
            term = lax.dot_general(
                cot_v[span, part], attn_v[span], (((0,), (0,)), ((), ())),
                preferred_element_type=jnp.float32,
            )
            if k > 0:
                term = total[part] + term
            if k < slabs - 1:
                total[part] = term
            else:
                put(first, term)


def product(attn_out, cotangent, token_count, orders, rows):
    tok_rows, width = attn_out.shape
    owned = sum(rows)
    features = cotangent.shape[1]
    slabs = 6 if tok_rows % 96 == 0 else 1
    far = [pltpu.with_memory_space_constraint(v, pltpu.HBM) for v in (attn_out, cotangent)]
    return pl.pallas_call(
        functools.partial(product_kernel, orders, rows, owned, slabs, max(256, owned)),
        out_shape=[
            jax.ShapeDtypeStruct((features // owned, r, width), jnp.float32) for r in rows
        ],
        in_specs=[pl.BlockSpec(memory_space=pltpu.SMEM)] + [pl.BlockSpec(memory_space=pltpu.HBM)] * 2,
        out_specs=[pl.BlockSpec(memory_space=pltpu.VMEM)] * len(rows),
        scratch_shapes=[
            pltpu.VMEM((tok_rows, width), attn_out.dtype),
            pltpu.VMEM((tok_rows, features), cotangent.dtype),
            pltpu.VMEM((features, width), jnp.float32),
            pltpu.SemaphoreType.DMA((slabs,)),
            pltpu.SemaphoreType.DMA((slabs,)),
        ],
        compiler_params=pltpu.CompilerParams(vmem_limit_bytes=32 * 1024 * 1024),
        cost_estimate=pl.CostEstimate(
            flops=2 * tok_rows * width * features,
            bytes_accessed=2 * tok_rows * (width + features) + 4 * width * features,
            transcendentals=0,
        ),
    )(token_count, *far)


def swap(value, pair, reps, devices):
    pairs = [
        (r * devices + f, r * devices + (f ^ pair[r % 2]))
        for r in range(reps) for f in range(devices)
    ]
    return lax.ppermute(value, ("rep", "fsdp"), pairs)


def local(attn_out, cotangent, numer, push_weight, moment1, moment2, step_index, token_count):
    owned = numer.shape[1]
    reps, devices = lax.axis_size("rep"), lax.axis_size("fsdp")
    count = token_count[0]
    orders, rows = orders_of(devices), rows_of(owned)
    blocks = product(attn_out, cotangent, token_count, orders, rows)

    send, keep = [b[devices // 2:] for b in blocks], [b[:devices // 2] for b in blocks]
    def mate_of(value):
        def exchange(bit, v):
            return lax.ppermute(v, "rep", [(r, r ^ (1 << bit)) for r in range(reps)])

        bit_count = reps.bit_length() - 1
        if bit_count == 1:
            return exchange(0, value)
        return lax.switch(
            step_index[0] % bit_count,
            [functools.partial(exchange, b) for b in range(bit_count)],
            value,
        )

    stages = devices.bit_length() - 1
    mixed_weight = 0.75 * push_weight + 0.25 * mate_of(push_weight)
    for k in range(stages):
        got = [swap(send[c], (orders[c][0][k], orders[c][1][k]), reps, devices) for c in range(len(orders))]
        if k == 0:
            got[0], mixed_weight = lax.optimization_barrier((got[0], mixed_weight))
        for c in range(len(orders)):
            if k < stages - 1:
                half = keep[c].shape[0] // 2
                send[c] = keep[c][half:] + got[c][half:]
                keep[c] = keep[c][:half] + got[c][:half]
            else:
                keep[c] = keep[c] + got[c]
    total = jnp.concatenate(keep, axis=1)
    grad = total / count.astype(jnp.float32)
    step = step_index[0]
    t_value = (step + 1).astype(jnp.float32)
    beta_one = jnp.float32(0.9)
    beta_two = jnp.float32(0.95)
    new_moment1 = beta_one * moment1 + (1.0 - beta_one) * grad
    new_moment2 = beta_two * moment2 + (1.0 - beta_two) * grad * grad
    weight_col = push_weight[:, None, None]
    debiased = numer / weight_col
    first_hat = new_moment1 / (1.0 - jnp.power(beta_one, t_value))
    second_hat = new_moment2 / (1.0 - jnp.power(beta_two, t_value))
    update = first_hat / (jnp.sqrt(second_hat) + 1e-08) + 0.1 * debiased
    stepped = numer - 0.02 * weight_col * update

    mate_numer = mate_of(stepped)
    mixed_numer = 0.75 * stepped + 0.25 * mate_numer
    return (mixed_numer, mixed_weight, new_moment1, new_moment2)


def solution(mesh):
    placed = (
        P(("rep", "fsdp"), None),
        P(("rep", "fsdp"), None),
        P("rep", "fsdp", None),
        P("rep"),
        P("rep", "fsdp", None),
        P("rep", "fsdp", None),
        P(),
        P("rep"),
    )
    return jax.shard_map(
        local,
        mesh=mesh,
        in_specs=placed,
        out_specs=(
            P("rep", "fsdp", None),
            P("rep"),
            P("rep", "fsdp", None),
            P("rep", "fsdp", None),
        ),
        check_vma=False,
    )
```

```python
import functools
import jax
import jax.numpy as jnp
from jax import lax
from jax.experimental import pallas as pl
from jax.experimental.pallas import tpu as pltpu
from jax.sharding import PartitionSpec as P

ORDERS = (
    ((1, 2, 4, 8), (8, 2, 1, 4)),
    ((2, 4, 8, 1), (4, 1, 2, 8)),
)
SHARE = 0.5


def orders_of(size):
    if size == 16:
        return ORDERS
    bits = tuple(1 << k for k in range(size.bit_length() - 1))
    turned = bits[1:] + bits[:1]
    return ((bits, turned), (bits[::-1], turned[::-1]))


def rows_of(owned):
    first = min(max(8, 8 * round(SHARE * owned / 8)), owned - 8)
    return (first, owned - first)


def place(relative, order):
    top = len(order) - 1
    spot = 0
    for k, bit in enumerate(order):
        low = bit.bit_length() - 1
        spot = spot | (((relative >> low) & 1) << (top - k))
    return spot


def product_kernel(orders, rows, owned, slabs, columns, count, attn, cot, *rest):
    outs = rest[:len(orders)]
    attn_v, cot_v, total, attn_sems, cot_sems = rest[len(orders):]
    tok_rows, width = attn.shape
    me, core = lax.axis_index("fsdp"), lax.axis_index("rep") % 2
    depth = tok_rows // slabs
    spans = [pl.ds(k * depth, depth) for k in range(slabs)]
    attn_in = [
        pltpu.make_async_copy(attn.at[span], attn_v.at[span], attn_sems.at[k])
        for k, span in enumerate(spans)
    ]
    cot_in = [
        pltpu.make_async_copy(cot.at[span], cot_v.at[span], cot_sems.at[k])
        for k, span in enumerate(spans)
    ]
    for k in range(slabs):
        attn_in[k].start()
        cot_in[k].start()
    live = count[0] - me * tok_rows

    def put(first, result):
        for s in range(columns // owned):
            relative = me ^ (first // owned + s)
            base = s * owned
            for c, (even, odd) in enumerate(orders):
                spot = jnp.where(core == 0, place(relative, even), place(relative, odd))
                outs[c][spot] = result[base:base + rows[c]]
                base += rows[c]

    for k, span in enumerate(spans):
        attn_in[k].wait()

        @pl.when(live < (k + 1) * depth)
        def _():
            position = k * depth + lax.broadcasted_iota(jnp.int32, (depth, width), 0)
            kept = jnp.where(position < live, attn_v[span].astype(jnp.float32), 0.0)
            attn_v[span] = kept.astype(attn_v.dtype)

        cot_in[k].wait()
        for first in range(0, cot.shape[1], columns):
            part = pl.ds(first, columns)
            term = lax.dot_general(
                cot_v[span, part], attn_v[span], (((0,), (0,)), ((), ())),
                preferred_element_type=jnp.float32,
            )
            if k > 0:
                term = total[part] + term
            if k < slabs - 1:
                total[part] = term
            else:
                put(first, term)


def product(attn_out, cotangent, token_count, orders, rows):
    tok_rows, width = attn_out.shape
    owned = sum(rows)
    features = cotangent.shape[1]
    slabs = 6 if tok_rows % 96 == 0 else 1
    far = [pltpu.with_memory_space_constraint(v, pltpu.HBM) for v in (attn_out, cotangent)]
    return pl.pallas_call(
        functools.partial(product_kernel, orders, rows, owned, slabs, max(256, owned)),
        out_shape=[
            jax.ShapeDtypeStruct((features // owned, r, width), jnp.float32) for r in rows
        ],
        in_specs=[pl.BlockSpec(memory_space=pltpu.SMEM)] + [pl.BlockSpec(memory_space=pltpu.HBM)] * 2,
        out_specs=[pl.BlockSpec(memory_space=pltpu.VMEM)] * len(rows),
        scratch_shapes=[
            pltpu.VMEM((tok_rows, width), attn_out.dtype),
            pltpu.VMEM((tok_rows, features), cotangent.dtype),
            pltpu.VMEM((features, width), jnp.float32),
            pltpu.SemaphoreType.DMA((slabs,)),
            pltpu.SemaphoreType.DMA((slabs,)),
        ],
        compiler_params=pltpu.CompilerParams(vmem_limit_bytes=32 * 1024 * 1024),
        cost_estimate=pl.CostEstimate(
            flops=2 * tok_rows * width * features,
            bytes_accessed=2 * tok_rows * (width + features) + 4 * width * features,
            transcendentals=0,
        ),
    )(token_count, *far)


def swap(value, pair, reps, devices):
    pairs = [
        (r * devices + f, r * devices + (f ^ pair[r % 2]))
        for r in range(reps) for f in range(devices)
    ]
    return lax.ppermute(value, ("rep", "fsdp"), pairs)


def local(attn_out, cotangent, numer, push_weight, moment1, moment2, step_index, token_count):
    owned = numer.shape[1]
    reps, devices = lax.axis_size("rep"), lax.axis_size("fsdp")
    count = token_count[0]
    orders, rows = orders_of(devices), rows_of(owned)
    blocks = product(attn_out, cotangent, token_count, orders, rows)

    send, keep = [b[devices // 2:] for b in blocks], [b[:devices // 2] for b in blocks]
    def mate_of(value):
        def exchange(bit, v):
            return lax.ppermute(v, "rep", [(r, r ^ (1 << bit)) for r in range(reps)])

        bit_count = reps.bit_length() - 1
        if bit_count == 1:
            return exchange(0, value)
        return lax.switch(
            step_index[0] % bit_count,
            [functools.partial(exchange, b) for b in range(bit_count)],
            value,
        )

    stages = devices.bit_length() - 1
    mixed_weight = 0.75 * push_weight + 0.25 * mate_of(push_weight)
    t_value = (step_index[0] + 1).astype(jnp.float32)
    beta_one = jnp.float32(0.9)
    beta_two = jnp.float32(0.95)
    one = 1.0 - jnp.power(beta_one, t_value)
    two = 1.0 - jnp.power(beta_two, t_value)
    for k in range(stages):
        got = [swap(send[c], (orders[c][0][k], orders[c][1][k]), reps, devices) for c in range(len(orders))]
        if k == 0:
            got[0], mixed_weight, one, two = lax.optimization_barrier(
                (got[0], mixed_weight, one, two)
            )
        for c in range(len(orders)):
            if k < stages - 1:
                half = keep[c].shape[0] // 2
                send[c] = keep[c][half:] + got[c][half:]
                keep[c] = keep[c][:half] + got[c][:half]
            else:
                keep[c] = keep[c] + got[c]
    total = jnp.concatenate(keep, axis=1)
    grad = total / count.astype(jnp.float32)
    new_moment1 = beta_one * moment1 + (1.0 - beta_one) * grad
    new_moment2 = beta_two * moment2 + (1.0 - beta_two) * grad * grad
    weight_col = push_weight[:, None, None]
    debiased = numer / weight_col
    first_hat = new_moment1 / one
    second_hat = new_moment2 / two
    update = first_hat / (jnp.sqrt(second_hat) + 1e-08) + 0.1 * debiased
    stepped = numer - 0.02 * weight_col * update

    mate_numer = mate_of(stepped)
    mixed_numer = 0.75 * stepped + 0.25 * mate_numer
    return (mixed_numer, mixed_weight, new_moment1, new_moment2)


def solution(mesh):
    placed = (
        P(("rep", "fsdp"), None),
        P(("rep", "fsdp"), None),
        P("rep", "fsdp", None),
        P("rep"),
        P("rep", "fsdp", None),
        P("rep", "fsdp", None),
        P(),
        P("rep"),
    )
    return jax.shard_map(
        local,
        mesh=mesh,
        in_specs=placed,
        out_specs=(
            P("rep", "fsdp", None),
            P("rep"),
            P("rep", "fsdp", None),
            P("rep", "fsdp", None),
        ),
        check_vma=False,
    )
```
